32 devices in a mesh: stream: 4 (over z), span: 2 (over y), radial: 4 (over x, core).
Axes of the slice: x: 2, y: 2, z: 4, core: 2. Of those that a mesh axis runs over, the one named last changes fastest.
Arguments:
- velocity: float32 [3, 32, 32, 1024], P(None, 'stream', 'span', 'radial'), may hold values from -6 to 6
- probe: float32 [8192, 128], P(('stream', 'span', 'radial')), may hold values from -6 to 6
- eddy: float32 [16384, 128], P(('stream', 'span', 'radial')), may hold values from 0.2 to 2.3
- slot_row: int32 [256, 64], P(('stream', 'span', 'radial')), may hold values from -1 to 255, as said below
- row_cell: int32 [8192], P(('stream', 'span', 'radial')), may hold values from 0 to 32767
Outputs:
- predicted: float32 [3, 32, 32, 1024], P(None, 'stream', 'span', 'radial')
- wall_stress: float32 [2, 8192], P(None, ('stream', 'span', 'radial'))
The draws below stay inside these ranges and needn't reach their ends.
Inputs may be any that keep to these rules, and one draw needn't show every extreme that they name: `slot_row`: for every tile, each of its exchange points 0 to 255 stands in exactly one slot of its 8 x 64 block; -1 marks an empty slot. In every draw some owner of each radial index has all 64 slots filled from every tile.
All inputs are finite; a program needn't handle non-finite values.
Results may differ from the reference program's by a relative error of at most 0.0003.
Values sent between devices are 32-bit elements; how exact they have to be, the bound alone decides.
A program may use at most 64 MiB of HBM per device.

```python
import math
import jax
import jax.numpy as jnp
from jax import lax

CX = 8
CY = 16
CZ = 256
ROWS_DEV = 256
NW = 64
ITERS = 6
NX = 32
NY = 32
NZ = 1024
OWNER_GROUP_SIZE = 8
TILES = 32
SLOTS_DEV = 512
CAP = 64
ROWS = 8192
SLOTS = 16384
N_STREAM = 4
N_SPAN = 2
N_RADIAL = 4


def draw_slot_row(key, part):
    shared_owner = jax.random.fold_in(key, 11)
    complete_random_key, extra_random_key = jax.random.split(shared_owner)
    radial_station_count = TILES // OWNER_GROUP_SIZE
    complete_owner = jax.random.randint(complete_random_key, (radial_station_count,), 0, OWNER_GROUP_SIZE)
    extra_weight = jax.random.randint(extra_random_key, (radial_station_count, OWNER_GROUP_SIZE), 0, 4)
    owner_of_slot = jnp.arange(SLOTS_DEV, dtype=jnp.int32) // CAP

    def one_tile(tile):
        local = jax.random.fold_in(jax.random.fold_in(key, 23), tile)
        radial_station = tile % radial_station_count
        random_jitter = jax.random.randint(local, (SLOTS_DEV,), 0, 2048)
        ranking_value = random_jitter + extra_weight[radial_station][owner_of_slot] * 2048 + jnp.where(owner_of_slot == complete_owner[radial_station], 16384, 0)
        distinct = ranking_value * SLOTS_DEV + jnp.arange(SLOTS_DEV, dtype=jnp.int32)
        chosen = lax.top_k(distinct, ROWS_DEV)[1]
        return jnp.full((SLOTS_DEV,), -1, jnp.int32).at[chosen].set(jnp.arange(ROWS_DEV, dtype=jnp.int32))
    table = jax.vmap(one_tile)(jnp.arange(TILES, dtype=jnp.int32))
    return table.reshape(TILES * OWNER_GROUP_SIZE, CAP)


def place_ends(values, own_key, least, largest):
    longest = values.shape.index(max(values.shape))
    spots = []
    for shift in (0, 1):
        where = [jax.random.randint(jax.random.fold_in(own_key, axis), (), 0, length) for axis, length in enumerate(values.shape)]
        where[longest] = (where[longest] + shift) % values.shape[longest]
        spots.append(tuple(where))
    return values.at[spots[0]].set(least).at[spots[1]].set(largest)


def steps_of(rng, extent, shards, smallest, top_value):
    factor_of, own = 1.0, jax.random.fold_in(rng, 6)
    for position, blocks in shards:
        steps = jnp.exp(jax.random.uniform(jax.random.fold_in(own, position), (blocks,), jnp.float32, smallest / len(shards), top_value / len(shards)))
        factor_of = factor_of * jnp.repeat(steps, extent[position] // blocks).reshape([-1 if axis == position else 1 for axis in range(len(extent))])
    return factor_of


def scatter_about(stream_key, dims, spread, most, shards=(), kind=jnp.bfloat16):
    drawn = spread * jax.random.normal(stream_key, dims, jnp.float32)
    if shards:
        drawn = drawn * steps_of(stream_key, dims, shards, -0.22, 0.18)
    return jnp.clip(drawn, -most, most).astype(kind)


def setup_inputs(seed: int = 0) -> dict:
    arg_keys = jax.random.split(jax.random.key(seed), 6)
    return {
        "velocity": scatter_about(arg_keys[0], (3, NX, NY, NZ), 1.0, 6.0, ((1, 4), (2, 2), (3, 4)), jnp.float32),
        "probe": scatter_about(arg_keys[1], (ROWS, 2 * NW), 1.0, 6.0, ((0, 32),), jnp.float32),
        "eddy": jnp.clip(jnp.exp(math.log(2.3) - 2.442347 * jax.random.uniform(arg_keys[2], (SLOTS, 2 * NW), jnp.float32) ** steps_of(arg_keys[2], (SLOTS, 2 * NW), ((0, 32),), -0.2, 0.2)), 0.2, 2.3),
        "slot_row": draw_slot_row(jax.random.fold_in(arg_keys[5], 71), 0),
        "row_cell": place_ends(jax.random.randint(arg_keys[4], (ROWS,), 0, CX * CY * CZ), jax.random.fold_in(arg_keys[4], 1), 0, (CX * CY * CZ) - 1).astype(jnp.int32),
    }


source_gain = 0.00390625
relaxation = 0.8
time_step = 0.1
diffusion = 0.5
wall_gain = 0.25


def green_table(points):
    left_index = lax.broadcasted_iota(jnp.int32, (2 * points, 2 * points), 0)
    right_index = lax.broadcasted_iota(jnp.int32, (2 * points, 2 * points), 1)
    left_pos = left_index % points
    right_pos = right_index % points
    same_part = (left_index // points) == (right_index // points)
    values = (jnp.minimum(left_pos, right_pos) + 1).astype(jnp.float32) * (points - jnp.maximum(left_pos, right_pos)).astype(jnp.float32) / (points + 1.0)
    return jnp.where(same_part, values, jnp.zeros_like(values))


def wall_solve(samples, viscosity):
    points = samples.shape[1] // 2
    column = lax.broadcasted_iota(jnp.int32, samples.shape, 1)
    height = column % points
    at_wall = height == 0
    at_top = height == points - 1
    visc_above = jnp.where(at_top, viscosity, jnp.roll(viscosity, -1, axis=1))
    source_term = source_gain * samples + jnp.where(at_top, viscosity * samples, jnp.zeros_like(samples))
    table = green_table(points)
    solution = jnp.zeros_like(samples)
    for sweep in range(ITERS):
        below_cell = jnp.where(at_wall, jnp.zeros_like(solution), jnp.roll(solution, 1, axis=1))
        above_cell = jnp.where(at_top, jnp.zeros_like(solution), jnp.roll(solution, -1, axis=1))
        applied = viscosity * (solution - below_cell) - visc_above * (above_cell - solution)
        solution = solution + relaxation * jnp.dot(source_term - applied, table, precision=lax.Precision.HIGHEST, preferred_element_type=jnp.float32)
    wall_values = (points + 1.0) * viscosity * solution
    return jnp.stack([wall_values[:, 0], wall_values[:, points]], axis=1)


def fluid(padded):
    center = padded[:, 1:-1, 1:-1, 1:-1]
    upper_x = padded[:, 2:, 1:-1, 1:-1]
    lower_x = padded[:, :-2, 1:-1, 1:-1]
    upper_y = padded[:, 1:-1, 2:, 1:-1]
    lower_y = padded[:, 1:-1, :-2, 1:-1]
    upper_z = padded[:, 1:-1, 1:-1, 2:]
    lower_z = padded[:, 1:-1, 1:-1, :-2]
    divergence = 0.5 * (upper_x * upper_x[0:1] - lower_x * lower_x[0:1] + upper_y * upper_y[1:2] - lower_y * lower_y[1:2] + upper_z * upper_z[2:3] - lower_z * lower_z[2:3])
    laplace = upper_x + lower_x + upper_y + lower_y + upper_z + lower_z - 6.0 * center
    return diffusion * laplace - divergence


def reference(velocity, probe, eddy, slot_row, row_cell):
    groups = N_STREAM * N_SPAN
    devices = N_STREAM * N_SPAN * N_RADIAL
    owner_eddy = eddy.reshape(groups, N_RADIAL, groups, CAP, 2 * NW)
    owner_eddy = jnp.transpose(owner_eddy, (2, 1, 0, 3, 4)).reshape(devices, groups * CAP, 2 * NW)
    slot_lists = slot_row.reshape(devices, groups * CAP)
    tile_rows = probe.reshape(devices, ROWS_DEV, 2 * NW)
    cell_lists = row_cell.reshape(devices, ROWS_DEV)

    def per_device(operands):
        slot_visc, slot_list, samples, cell_list = operands
        target = jnp.where(slot_list >= 0, slot_list, ROWS_DEV).astype(jnp.int32)
        viscosity = jnp.zeros((ROWS_DEV, 2 * NW), jnp.float32).at[target].set(slot_visc, mode="drop")
        stress = wall_solve(samples, viscosity)
        forcing_tile = jnp.zeros((CX * CY * CZ, 2), jnp.float32).at[cell_list.astype(jnp.int32)].add(stress)
        return forcing_tile, stress

    forcing, stresses = lax.map(per_device, (owner_eddy, slot_lists, tile_rows, cell_lists))
    wall_stress = jnp.transpose(stresses.reshape(devices * ROWS_DEV, 2))
    forcing = forcing.reshape(N_STREAM, N_SPAN, N_RADIAL, CX, CY, CZ, 2)
    forcing = jnp.transpose(forcing, (6, 0, 3, 1, 4, 2, 5)).reshape(2, NX, NY, NZ)
    padded = jnp.pad(velocity, ((0, 0), (1, 1), (1, 1), (1, 1)))
    predicted = velocity + time_step * fluid(padded)
    predicted = jnp.concatenate([predicted[0:2] - wall_gain * forcing, predicted[2:3]], axis=0)
    return predicted, wall_stress
```

```python
import functools
import jax
import jax.numpy as jnp
from jax import lax
from jax.experimental import pallas as pl
from jax.experimental.pallas import tpu as pltpu
from jax.sharding import PartitionSpec as P

ITERS = 6

source_gain = 0.00390625
relaxation = 0.8
time_step = 0.1
diffusion = 0.5
wall_gain = 0.25

MESH = pl.DeviceIdType.MESH


def halves(x):
    high = x.astype(jnp.bfloat16)
    return high, (x - high.astype(jnp.float32)).astype(jnp.bfloat16)


def dot(a, b, dims):
    return lax.dot_general(a, b, (dims, ((), ())), preferred_element_type=jnp.float32)


def suffix_sums(samples):
    width = samples.shape[1]
    points = width // 2
    row = lax.broadcasted_iota(jnp.int32, (width, width), 0)
    col = lax.broadcasted_iota(jnp.int32, (width, width), 1)
    keep = (col >= row) & ((col >= points) == (row >= points))
    table = jnp.where(keep, source_gain, 0.0).astype(jnp.bfloat16)
    high, low = halves(samples)
    return dot(table, high, ((1,), (1,))) + dot(table, low, ((1,), (1,)))


def wall_solve(visc, w):
    points, count = visc.shape[1], visc.shape[1] + 1
    v_top = visc[:, points - 1 : points]
    w_top = -(v_top * (w[:, points - 1 : points] * (1.0 / source_gain)))
    u, u_top = w, w_top
    d = jnp.zeros_like(w)
    d_top = jnp.zeros_like(w_top)
    for sweep in range(ITERS):
        mean = (jnp.sum(u, axis=1, keepdims=True) + u_top) * (1.0 / count)
        if sweep == ITERS - 1:
            first = d[:, 0:1] + relaxation * (u[:, 0:1] - mean)
            return (count * visc[:, 0:1] * first)[:, 0]
        d = d + relaxation * (u - mean)
        d_top = d_top + relaxation * (u_top - mean)
        u = w - visc * d
        u_top = w_top - v_top * d_top


def kernel(
    sizes, vel, probe_far, eddy, slots_far, cells_far, out, stress_out,
    vpad, recv, probe, slots, cells, y_out, y_in, z_out, z_in,
    send_sem, recv_sem, halo_send, halo_recv, local_sem,
):
    n_stream, n_span, n_radial = sizes
    s, p, r = (lax.axis_index(a) for a in ("stream", "span", "radial"))
    groups, capacity, width = eddy.shape
    _, cx, cy, cz = vel.shape
    me = s * n_span + p

    def partner(k):
        g = lax.rem(me + k, groups)
        return g, (lax.div(g, n_span), lax.rem(g, n_span), r)

    load = pltpu.make_async_copy(vel, vpad.at[:, pl.ds(1, cx)], local_sem.at[0])
    load.start()
    smalls = [
        pltpu.make_async_copy(far, near, local_sem.at[2 + i])
        for i, (far, near) in enumerate(((probe_far, probe), (slots_far, slots), (cells_far, cells)))
    ]
    for copy in smalls:
        copy.start()
    own = pltpu.make_async_copy(eddy.at[me], recv.at[me], local_sem.at[1])
    own.start()

    barrier = pltpu.get_barrier_semaphore()

    def greet(k, carry):
        pl.semaphore_signal(barrier, inc=1, device_id=partner(k)[1], device_id_type=MESH)
        return carry

    lax.fori_loop(1, groups, greet, 0)

    for radial in (lax.rem(r + 1, n_radial), lax.rem(r + n_radial - 1, n_radial)):
        pl.semaphore_signal(barrier, inc=1, device_id=(s, p, radial), device_id_type=MESH)
    pl.semaphore_wait(barrier, groups + 1)

    def eddy_copy(k):
        g, device = partner(k)
        return pltpu.make_async_remote_copy(
            src_ref=eddy.at[g], dst_ref=recv.at[me], send_sem=send_sem.at[g],
            recv_sem=recv_sem.at[me], device_id=device, device_id_type=MESH,
        )

    def send(k, carry):
        eddy_copy(k).start()
        return carry

    lax.fori_loop(1, groups, send, 0)

    load.wait()

    def faces():
        def copy(i, src, dst, device):
            return pltpu.make_async_remote_copy(
                src_ref=src, dst_ref=dst, send_sem=halo_send.at[i],
                recv_sem=halo_recv.at[i], device_id=device, device_id_type=MESH,
            )
        return [
            (s < n_stream - 1, s > 0, copy(0, vpad.at[:, cx], vpad.at[:, 0], (s + 1, p, r))),
            (s > 0, s < n_stream - 1, copy(1, vpad.at[:, 1], vpad.at[:, cx + 1], (s - 1, p, r))),
            (p < n_span - 1, p > 0, copy(2, y_out.at[0], y_in.at[0], (s, p + 1, r))),
            (p > 0, p < n_span - 1, copy(3, y_out.at[1], y_in.at[1], (s, p - 1, r))),
            (r < n_radial - 1, r > 0, copy(4, z_out.at[0], z_in.at[0], (s, p, r + 1))),
            (r > 0, r < n_radial - 1, copy(5, z_out.at[1], z_in.at[1], (s, p, r - 1))),
        ]

    sides = faces()
    fills = [vpad.at[:, 0], vpad.at[:, cx + 1], y_in.at[0], y_in.at[1], z_in.at[0], z_in.at[1]]
    for i in (0, 1):
        pl.when(sides[i][0])(sides[i][2].start)

    y_out[0] = vpad[:, 1 : cx + 1, cy - 1 : cy, :]
    y_out[1] = vpad[:, 1 : cx + 1, 0:1, :]
    for i in (2, 3):
        pl.when(sides[i][0])(sides[i][2].start)

    lanes = z_out.shape[2]
    shape4 = (3, cx, cy, lanes)
    plane = lax.broadcasted_iota(jnp.int32, shape4, 0) * cx + lax.broadcasted_iota(jnp.int32, shape4, 1)
    picked = plane == lax.broadcasted_iota(jnp.int32, shape4, 3)
    for i, column in ((0, cz - 1), (1, 0)):
        face = jnp.where(picked, vpad[:, 1 : cx + 1, :, column : column + 1], 0.0)
        z_out[i] = jnp.sum(jnp.sum(face, axis=0), axis=0)
    for i in (4, 5):
        pl.when(sides[i][0])(sides[i][2].start)

    for (_, arrives, _), ref in zip(sides, fills):
        @pl.when(jnp.logical_not(arrives))
        def _():
            ref[...] = jnp.zeros(ref.shape, ref.dtype)

    rows = probe.shape[0]
    for copy in smalls:
        copy.wait()
    w = suffix_sums(probe[...])
    if slots.shape[0] == 1:
        slot_line = slots[...]
    else:
        slot_line = jnp.concatenate([slots[g : g + 1, :] for g in range(groups)], axis=1)
    total = groups * capacity
    place = (lax.broadcasted_iota(jnp.int32, (rows, total), 0) == slot_line).astype(jnp.float32).astype(jnp.bfloat16)
    cell = cells[...]
    cell_z = lax.rem(cell, cz)
    cell_xy = lax.div(cell, cz)
    at_z = (lax.broadcasted_iota(jnp.int32, (cz, rows), 0) == cell_z).astype(jnp.float32).astype(jnp.bfloat16)

    for _, arrives, copy in sides:
        pl.when(arrives)(copy.wait_recv)

    line = lax.broadcasted_iota(jnp.int32, (3, cy, cz), 1)
    lane = lax.broadcasted_iota(jnp.int32, (3, cy, cz), 2)
    spot = lax.broadcasted_iota(jnp.int32, (3, cy, lanes), 0) * cx
    spot_lane = lax.broadcasted_iota(jnp.int32, (3, cy, lanes), 2)

    def step(x, carry):
        center = vpad[:, x + 1]
        lower_x = vpad[:, x]
        upper_x = vpad[:, x + 2]
        lower_y = jnp.where(line == 0, y_in[0, :, x], pltpu.roll(center, 1, 1))
        upper_y = jnp.where(line == cy - 1, y_in[1, :, x], pltpu.roll(center, cy - 1, 1))
        here = spot + x == spot_lane
        low_z = jnp.sum(jnp.where(here, z_in[0][None], 0.0), axis=2, keepdims=True)
        high_z = jnp.sum(jnp.where(here, z_in[1][None], 0.0), axis=2, keepdims=True)
        lower_z = jnp.where(lane == 0, low_z, pltpu.roll(center, 1, 2))
        upper_z = jnp.where(lane == cz - 1, high_z, pltpu.roll(center, cz - 1, 2))
        divergence = 0.5 * (
            upper_x * upper_x[0:1] - lower_x * lower_x[0:1]
            + upper_y * upper_y[1:2] - lower_y * lower_y[1:2]
            + upper_z * upper_z[2:3] - lower_z * lower_z[2:3]
        )
        laplace = upper_x + lower_x + upper_y + lower_y + upper_z + lower_z - 6.0 * center
        out[:, x] = center + time_step * (diffusion * laplace - divergence)
        return carry

    lax.fori_loop(0, cx, step, 0)

    own.wait()

    def arrived(k, carry):
        g, device = partner(k)
        pltpu.make_async_remote_copy(
            src_ref=eddy.at[g], dst_ref=recv.at[g], send_sem=send_sem.at[g],
            recv_sem=recv_sem.at[g], device_id=device, device_id_type=MESH,
        ).wait_recv()
        return carry

    lax.fori_loop(1, groups, arrived, 0)

    high, low = halves(recv[...].reshape(total, width))
    visc = dot(place, high, ((1,), (0,))) + dot(place, low, ((1,), (0,)))
    visc = jnp.transpose(visc).reshape(2, width // 2, rows)
    stress = wall_solve(visc, w.reshape(2, width // 2, rows))
    stress_out[...] = stress

    at_xy = lax.broadcasted_iota(jnp.int32, (cx * cy, rows), 0) == cell_xy
    for c in range(2):
        high, low = halves(jnp.where(at_xy, wall_gain * stress[c : c + 1], 0.0))
        forcing = dot(high, at_z, ((1,), (1,))) + dot(low, at_z, ((1,), (1,)))
        out[c] = out[c] - forcing.reshape(cx, cy, cz)

    for leaves, _, copy in sides:
        pl.when(leaves)(copy.wait_send)

    def sent(k, carry):
        eddy_copy(k).wait_send()
        return carry

    lax.fori_loop(1, groups, sent, 0)


def shards(sizes, velocity, probe, eddy, slot_row, row_cell):
    groups, capacity = slot_row.shape
    rows, width = probe.shape
    _, cx, cy, cz = velocity.shape
    if capacity % 8:
        slot_row = slot_row.reshape(1, groups * capacity)
    f32 = jnp.float32
    vmem = pl.BlockSpec(memory_space=pltpu.VMEM)
    hbm = pl.BlockSpec(memory_space=pltpu.HBM)
    return pl.pallas_call(
        functools.partial(kernel, sizes),
        out_shape=(
            jax.ShapeDtypeStruct(velocity.shape, f32),
            jax.ShapeDtypeStruct((2, rows), f32),
        ),
        in_specs=[hbm] * 5,
        out_specs=(vmem, vmem),
        scratch_shapes=[
            pltpu.VMEM((3, cx + 2, cy, cz), f32),
            pltpu.VMEM((groups, capacity, width), f32),
            pltpu.VMEM((rows, width), f32),
            pltpu.VMEM(slot_row.shape, jnp.int32),
            pltpu.VMEM((1, rows), jnp.int32),
            pltpu.VMEM((2, 3, cx, 1, cz), f32),
            pltpu.VMEM((2, 3, cx, 1, cz), f32),
            pltpu.VMEM((2, cy, 128), f32),
            pltpu.VMEM((2, cy, 128), f32),
            pltpu.SemaphoreType.DMA((groups,)),
            pltpu.SemaphoreType.DMA((groups,)),
            pltpu.SemaphoreType.DMA((6,)),
            pltpu.SemaphoreType.DMA((6,)),
            pltpu.SemaphoreType.DMA((5,)),
        ],
        compiler_params=pltpu.CompilerParams(
            collective_id=0, has_side_effects=True, vmem_limit_bytes=32 * 1024 * 1024
        ),
    )(velocity, probe, eddy.reshape(groups, capacity, width), slot_row, row_cell.reshape(1, rows))


def solution(mesh):
    in_specs = (
        P(None, "stream", "span", "radial"),
        P(("stream", "span", "radial"), None),
        P(("stream", "span", "radial"), None),
        P(("stream", "span", "radial"), None),
        P(("stream", "span", "radial")),
    )
    out_specs = (P(None, "stream", "span", "radial"), P(None, ("stream", "span", "radial")))
    sizes = tuple(mesh.shape[a] for a in ("stream", "span", "radial"))
    return jax.shard_map(
        functools.partial(shards, sizes), mesh=mesh, in_specs=in_specs, out_specs=out_specs, check_vma=False
    )
```

```python
import functools
import jax
import jax.numpy as jnp
from jax import lax
from jax.experimental import pallas as pl
from jax.experimental.pallas import tpu as pltpu
from jax.sharding import PartitionSpec as P

ITERS = 6

source_gain = 0.00390625
relaxation = 0.8
time_step = 0.1
diffusion = 0.5
wall_gain = 0.25

MESH = pl.DeviceIdType.MESH


def halves(x):
    high = x.astype(jnp.bfloat16)
    return high, (x - high.astype(jnp.float32)).astype(jnp.bfloat16)


def dot(a, b, dims):
    return lax.dot_general(a, b, (dims, ((), ())), preferred_element_type=jnp.float32)


def suffix_sums(samples):
    width = samples.shape[1]
    points = width // 2
    row = lax.broadcasted_iota(jnp.int32, (width, width), 0)
    col = lax.broadcasted_iota(jnp.int32, (width, width), 1)
    keep = (col >= row) & ((col >= points) == (row >= points))
    table = jnp.where(keep, source_gain, 0.0).astype(jnp.bfloat16)
    high, low = halves(samples)
    return dot(table, high, ((1,), (1,))) + dot(table, low, ((1,), (1,)))


def wall_solve(visc, w):
    points, count = visc.shape[1], visc.shape[1] + 1
    v_top = visc[:, points - 1 : points]
    w_top = -(v_top * (w[:, points - 1 : points] * (1.0 / source_gain)))
    u, u_top = w, w_top
    d = jnp.zeros_like(w)
    d_top = jnp.zeros_like(w_top)
    for sweep in range(ITERS):
        mean = (jnp.sum(u, axis=1, keepdims=True) + u_top) * (1.0 / count)
        if sweep == ITERS - 1:
            first = d[:, 0:1] + relaxation * (u[:, 0:1] - mean)
            return (count * visc[:, 0:1] * first)[:, 0]
        d = d + relaxation * (u - mean)
        d_top = d_top + relaxation * (u_top - mean)
        u = w - visc * d
        u_top = w_top - v_top * d_top


def kernel(
    sizes, vel, probe_far, eddy, slots_far, cells_far, out, stress_out,
    vpad, recv, probe, slots, cells, y_out, y_in, z_out, z_in,
    send_sem, recv_sem, halo_send, halo_recv, local_sem,
):
    n_stream, n_span, n_radial = sizes
    s, p, r = (lax.axis_index(a) for a in ("stream", "span", "radial"))
    groups, capacity, width = eddy.shape
    _, cx, cy, cz = vel.shape
    me = s * n_span + p

    def partner(k):
        g = lax.rem(me + k, groups)
        return g, (lax.div(g, n_span), lax.rem(g, n_span), r)

    load = pltpu.make_async_copy(vel, vpad.at[:, pl.ds(1, cx)], local_sem.at[0])
    load.start()
    smalls = [
        pltpu.make_async_copy(far, near, local_sem.at[2 + i])
        for i, (far, near) in enumerate(((probe_far, probe), (slots_far, slots), (cells_far, cells)))
    ]
    for copy in smalls:
        copy.start()
    own = pltpu.make_async_copy(eddy.at[me], recv.at[me], local_sem.at[1])
    own.start()

    barrier = pltpu.get_barrier_semaphore()

    def greet(k, carry):
        pl.semaphore_signal(barrier, inc=1, device_id=partner(k)[1], device_id_type=MESH)
        return carry

    lax.fori_loop(1, groups, greet, 0)

    for radial in (lax.rem(r + 1, n_radial), lax.rem(r + n_radial - 1, n_radial)):
        pl.semaphore_signal(barrier, inc=1, device_id=(s, p, radial), device_id_type=MESH)
    load.wait()
    y_out[0] = vpad[:, 1 : cx + 1, cy - 1 : cy, :]
    y_out[1] = vpad[:, 1 : cx + 1, 0:1, :]
    lanes = z_out.shape[2]
    shape4 = (3, cx, cy, lanes)
    plane = lax.broadcasted_iota(jnp.int32, shape4, 0) * cx + lax.broadcasted_iota(jnp.int32, shape4, 1)
    picked = plane == lax.broadcasted_iota(jnp.int32, shape4, 3)
    for i, column in ((0, cz - 1), (1, 0)):
        face = jnp.where(picked, vpad[:, 1 : cx + 1, :, column : column + 1], 0.0)
        z_out[i] = jnp.sum(jnp.sum(face, axis=0), axis=0)

    def face_copy(i, src, dst, device):
        return pltpu.make_async_remote_copy(
            src_ref=src, dst_ref=dst, send_sem=halo_send.at[i],
            recv_sem=halo_recv.at[i], device_id=device, device_id_type=MESH,
        )

    sides = [
        (s < n_stream - 1, s > 0, face_copy(0, vpad.at[:, cx], vpad.at[:, 0], (s + 1, p, r)), vpad.at[:, 0]),
        (s > 0, s < n_stream - 1, face_copy(1, vpad.at[:, 1], vpad.at[:, cx + 1], (s - 1, p, r)), vpad.at[:, cx + 1]),
        (p < n_span - 1, p > 0, face_copy(2, y_out.at[0], y_in.at[0], (s, p + 1, r)), y_in.at[0]),
        (p > 0, p < n_span - 1, face_copy(3, y_out.at[1], y_in.at[1], (s, p - 1, r)), y_in.at[1]),
        (r < n_radial - 1, r > 0, face_copy(4, z_out.at[0], z_in.at[0], (s, p, r + 1)), z_in.at[0]),
        (r > 0, r < n_radial - 1, face_copy(5, z_out.at[1], z_in.at[1], (s, p, r - 1)), z_in.at[1]),
    ]
    for _, arrives, _, ref in sides:
        @pl.when(jnp.logical_not(arrives))
        def _():
            ref[...] = jnp.zeros(ref.shape, ref.dtype)

    pl.semaphore_wait(barrier, groups + 1)

    def eddy_copy(k):
        g, device = partner(k)
        return pltpu.make_async_remote_copy(
            src_ref=eddy.at[g], dst_ref=recv.at[me], send_sem=send_sem.at[g],
            recv_sem=recv_sem.at[me], device_id=device, device_id_type=MESH,
        )

    def send(k, carry):
        eddy_copy(k).start()
        return carry

    lax.fori_loop(1, groups, send, 0)

    for leaves, _, copy, _ in sides:
        pl.when(leaves)(copy.start)

    rows = probe.shape[0]
    for copy in smalls:
        copy.wait()
    w = suffix_sums(probe[...])
    if slots.shape[0] == 1:
        slot_line = slots[...]
    else:
        slot_line = jnp.concatenate([slots[g : g + 1, :] for g in range(groups)], axis=1)
    total = groups * capacity
    place = (lax.broadcasted_iota(jnp.int32, (rows, total), 0) == slot_line).astype(jnp.float32).astype(jnp.bfloat16)
    cell = cells[...]
    cell_z = lax.rem(cell, cz)
    cell_xy = lax.div(cell, cz)
    at_z = (lax.broadcasted_iota(jnp.int32, (cz, rows), 0) == cell_z).astype(jnp.float32).astype(jnp.bfloat16)

    for _, arrives, copy, _ in sides:
        pl.when(arrives)(copy.wait_recv)

    line = lax.broadcasted_iota(jnp.int32, (3, cy, cz), 1)
    lane = lax.broadcasted_iota(jnp.int32, (3, cy, cz), 2)
    spot = lax.broadcasted_iota(jnp.int32, (3, cy, lanes), 0) * cx
    spot_lane = lax.broadcasted_iota(jnp.int32, (3, cy, lanes), 2)

    def step(x, carry):
        center = vpad[:, x + 1]
        lower_x = vpad[:, x]
        upper_x = vpad[:, x + 2]
        lower_y = jnp.where(line == 0, y_in[0, :, x], pltpu.roll(center, 1, 1))
        upper_y = jnp.where(line == cy - 1, y_in[1, :, x], pltpu.roll(center, cy - 1, 1))
        here = spot + x == spot_lane
        low_z = jnp.sum(jnp.where(here, z_in[0][None], 0.0), axis=2, keepdims=True)
        high_z = jnp.sum(jnp.where(here, z_in[1][None], 0.0), axis=2, keepdims=True)
        lower_z = jnp.where(lane == 0, low_z, pltpu.roll(center, 1, 2))
        upper_z = jnp.where(lane == cz - 1, high_z, pltpu.roll(center, cz - 1, 2))
        divergence = 0.5 * (
            upper_x * upper_x[0:1] - lower_x * lower_x[0:1]
            + upper_y * upper_y[1:2] - lower_y * lower_y[1:2]
            + upper_z * upper_z[2:3] - lower_z * lower_z[2:3]
        )
        laplace = upper_x + lower_x + upper_y + lower_y + upper_z + lower_z - 6.0 * center
        out[:, x] = center + time_step * (diffusion * laplace - divergence)
        return carry

    lax.fori_loop(0, cx, step, 0)

    own.wait()

    def arrived(k, carry):
        g, device = partner(k)
        pltpu.make_async_remote_copy(
            src_ref=eddy.at[g], dst_ref=recv.at[g], send_sem=send_sem.at[g],
            recv_sem=recv_sem.at[g], device_id=device, device_id_type=MESH,
        ).wait_recv()
        return carry

    lax.fori_loop(1, groups, arrived, 0)

    high, low = halves(recv[...].reshape(total, width))
    visc = dot(place, high, ((1,), (0,))) + dot(place, low, ((1,), (0,)))
    visc = jnp.transpose(visc).reshape(2, width // 2, rows)
    stress = wall_solve(visc, w.reshape(2, width // 2, rows))
    stress_out[...] = stress

    at_xy = lax.broadcasted_iota(jnp.int32, (cx * cy, rows), 0) == cell_xy
    for c in range(2):
        high, low = halves(jnp.where(at_xy, wall_gain * stress[c : c + 1], 0.0))
        forcing = dot(high, at_z, ((1,), (1,))) + dot(low, at_z, ((1,), (1,)))
        out[c] = out[c] - forcing.reshape(cx, cy, cz)

    for leaves, _, copy, _ in sides:
        pl.when(leaves)(copy.wait_send)

    def sent(k, carry):
        eddy_copy(k).wait_send()
        return carry

    lax.fori_loop(1, groups, sent, 0)


def shards(sizes, velocity, probe, eddy, slot_row, row_cell):
    groups, capacity = slot_row.shape
    rows, width = probe.shape
    _, cx, cy, cz = velocity.shape
    if capacity % 8:
        slot_row = slot_row.reshape(1, groups * capacity)
    f32 = jnp.float32
    vmem = pl.BlockSpec(memory_space=pltpu.VMEM)
    hbm = pl.BlockSpec(memory_space=pltpu.HBM)
    return pl.pallas_call(
        functools.partial(kernel, sizes),
        out_shape=(
            jax.ShapeDtypeStruct(velocity.shape, f32),
            jax.ShapeDtypeStruct((2, rows), f32),
        ),
        in_specs=[hbm] * 5,
        out_specs=(vmem, vmem),
        scratch_shapes=[
            pltpu.VMEM((3, cx + 2, cy, cz), f32),
            pltpu.VMEM((groups, capacity, width), f32),
            pltpu.VMEM((rows, width), f32),
            pltpu.VMEM(slot_row.shape, jnp.int32),
            pltpu.VMEM((1, rows), jnp.int32),
            pltpu.VMEM((2, 3, cx, 1, cz), f32),
            pltpu.VMEM((2, 3, cx, 1, cz), f32),
            pltpu.VMEM((2, cy, 128), f32),
            pltpu.VMEM((2, cy, 128), f32),
            pltpu.SemaphoreType.DMA((groups,)),
            pltpu.SemaphoreType.DMA((groups,)),
            pltpu.SemaphoreType.DMA((6,)),
            pltpu.SemaphoreType.DMA((6,)),
            pltpu.SemaphoreType.DMA((5,)),
        ],
        compiler_params=pltpu.CompilerParams(
            collective_id=0, has_side_effects=True
        ),
    )(velocity, probe, eddy.reshape(groups, capacity, width), slot_row, row_cell.reshape(1, rows))


def solution(mesh):
    in_specs = (
        P(None, "stream", "span", "radial"),
        P(("stream", "span", "radial"), None),
        P(("stream", "span", "radial"), None),
        P(("stream", "span", "radial"), None),
        P(("stream", "span", "radial")),
    )
    out_specs = (P(None, "stream", "span", "radial"), P(None, ("stream", "span", "radial")))
    sizes = tuple(mesh.shape[a] for a in ("stream", "span", "radial"))
    return jax.shard_map(
        functools.partial(shards, sizes), mesh=mesh, in_specs=in_specs, out_specs=out_specs, check_vma=False
    )
```

```python
import functools
import jax
import jax.numpy as jnp
from jax import lax
from jax.experimental import pallas as pl
from jax.experimental.pallas import tpu as pltpu
from jax.sharding import PartitionSpec as P

ITERS = 6

source_gain = 0.00390625
relaxation = 0.8
time_step = 0.1
diffusion = 0.5
wall_gain = 0.25

MESH = pl.DeviceIdType.MESH


def halves(x):
    high = x.astype(jnp.bfloat16)
    return high, (x - high.astype(jnp.float32)).astype(jnp.bfloat16)


def dot(a, b, dims):
    return lax.dot_general(a, b, (dims, ((), ())), preferred_element_type=jnp.float32)


def suffix_sums(samples):
    width = samples.shape[1]
    points = width // 2
    row = lax.broadcasted_iota(jnp.int32, (width, width), 0)
    col = lax.broadcasted_iota(jnp.int32, (width, width), 1)
    keep = (col >= row) & ((col >= points) == (row >= points))
    table = jnp.where(keep, source_gain, 0.0).astype(jnp.bfloat16)
    high, low = halves(samples)
    return dot(table, high, ((1,), (1,))) + dot(table, low, ((1,), (1,)))


def wall_solve(visc, w):
    points, count = visc.shape[1], visc.shape[1] + 1
    v_top = visc[:, points - 1 : points]
    w_top = -(v_top * (w[:, points - 1 : points] * (1.0 / source_gain)))
    u, u_top = w, w_top
    d = jnp.zeros_like(w)
    d_top = jnp.zeros_like(w_top)
    for sweep in range(ITERS):
        mean = (jnp.sum(u, axis=1, keepdims=True) + u_top) * (1.0 / count)
        if sweep == ITERS - 1:
            first = d[:, 0:1] + relaxation * (u[:, 0:1] - mean)
            return (count * visc[:, 0:1] * first)[:, 0]
        d = d + relaxation * (u - mean)
        d_top = d_top + relaxation * (u_top - mean)
        u = w - visc * d
        u_top = w_top - v_top * d_top


def kernel(
    sizes, vel, probe_far, eddy, slots_far, cells_far, out, stress_out,
    vpad, recv, probe, slots, cells, y_out, y_in, z_out, z_in,
    send_sem, recv_sem, halo_send, halo_recv, local_sem,
):
    n_stream, n_span, n_radial = sizes
    s, p, r = (lax.axis_index(a) for a in ("stream", "span", "radial"))
    groups, capacity, width = eddy.shape
    _, cx, cy, cz = vel.shape
    me = s * n_span + p

    def partner(k):
        g = lax.rem(me + k, groups)
        return g, (lax.div(g, n_span), lax.rem(g, n_span), r)

    load = pltpu.make_async_copy(vel, vpad.at[:, pl.ds(1, cx)], local_sem.at[0])
    load.start()
    smalls = [
        pltpu.make_async_copy(far, near, local_sem.at[2 + i])
        for i, (far, near) in enumerate(((probe_far, probe), (slots_far, slots), (cells_far, cells)))
    ]
    for copy in smalls:
        copy.start()
    own = pltpu.make_async_copy(eddy.at[me], recv.at[me], local_sem.at[1])
    own.start()

    barrier = pltpu.get_barrier_semaphore()

    def greet(k, carry):
        pl.semaphore_signal(barrier, inc=1, device_id=partner(k)[1], device_id_type=MESH)
        return carry

    lax.fori_loop(1, groups, greet, 0)

    for radial in (lax.rem(r + 1, n_radial), lax.rem(r + n_radial - 1, n_radial)):
        pl.semaphore_signal(barrier, inc=1, device_id=(s, p, radial), device_id_type=MESH)
    load.wait()
    y_out[0] = vpad[:, 1 : cx + 1, cy - 1 : cy, :]
    y_out[1] = vpad[:, 1 : cx + 1, 0:1, :]
    lanes = z_out.shape[2]
    shape4 = (3, cx, cy, lanes)
    plane = lax.broadcasted_iota(jnp.int32, shape4, 0) * cx + lax.broadcasted_iota(jnp.int32, shape4, 1)
    picked = plane == lax.broadcasted_iota(jnp.int32, shape4, 3)
    for i, column in ((0, cz - 1), (1, 0)):
        face = jnp.where(picked, vpad[:, 1 : cx + 1, :, column : column + 1], 0.0)
        z_out[i] = jnp.sum(jnp.sum(face, axis=0), axis=0)

    def face_copy(i, src, dst, device):
        return pltpu.make_async_remote_copy(
            src_ref=src, dst_ref=dst, send_sem=halo_send.at[i],
            recv_sem=halo_recv.at[i], device_id=device, device_id_type=MESH,
        )

    sides = [
        (s < n_stream - 1, s > 0, face_copy(0, vpad.at[:, cx], vpad.at[:, 0], (s + 1, p, r)), vpad.at[:, 0]),
        (s > 0, s < n_stream - 1, face_copy(1, vpad.at[:, 1], vpad.at[:, cx + 1], (s - 1, p, r)), vpad.at[:, cx + 1]),
        (p < n_span - 1, p > 0, face_copy(2, y_out.at[0], y_in.at[0], (s, p + 1, r)), y_in.at[0]),
        (p > 0, p < n_span - 1, face_copy(3, y_out.at[1], y_in.at[1], (s, p - 1, r)), y_in.at[1]),
        (r < n_radial - 1, r > 0, face_copy(4, z_out.at[0], z_in.at[0], (s, p, r + 1)), z_in.at[0]),
        (r > 0, r < n_radial - 1, face_copy(5, z_out.at[1], z_in.at[1], (s, p, r - 1)), z_in.at[1]),
    ]
    for _, arrives, _, ref in sides:
        @pl.when(jnp.logical_not(arrives))
        def _():
            ref[...] = jnp.zeros(ref.shape, ref.dtype)

    pl.semaphore_wait(barrier, groups + 1)

    def eddy_copy(k):
        g, device = partner(k)
        return pltpu.make_async_remote_copy(
            src_ref=eddy.at[g], dst_ref=recv.at[me], send_sem=send_sem.at[g],
            recv_sem=recv_sem.at[me], device_id=device, device_id_type=MESH,
        )

    def send(k, carry):
        eddy_copy(k).start()
        return carry

    lax.fori_loop(1, groups, send, 0)

    for leaves, _, copy, _ in sides:
        pl.when(leaves)(copy.start)

    rows = probe.shape[0]
    for copy in smalls:
        copy.wait()
    w = suffix_sums(probe[...])
    if slots.shape[0] == 1:
        slot_line = slots[...]
    else:
        slot_line = jnp.concatenate([slots[g : g + 1, :] for g in range(groups)], axis=1)
    total = groups * capacity
    place = (lax.broadcasted_iota(jnp.int32, (rows, total), 0) == slot_line).astype(jnp.float32).astype(jnp.bfloat16)
    cell = cells[...]
    cell_z = lax.rem(cell, cz)
    cell_xy = lax.div(cell, cz)
    at_z = (lax.broadcasted_iota(jnp.int32, (cz, rows), 0) == cell_z).astype(jnp.float32).astype(jnp.bfloat16)

    for _, arrives, copy, _ in sides:
        pl.when(arrives)(copy.wait_recv)

    line = lax.broadcasted_iota(jnp.int32, (3, cy, cz), 1)
    lane = lax.broadcasted_iota(jnp.int32, (3, cy, cz), 2)
    spot = lax.broadcasted_iota(jnp.int32, (3, cy, lanes), 0) * cx
    spot_lane = lax.broadcasted_iota(jnp.int32, (3, cy, lanes), 2)

    def step(x, carry):
        center = vpad[:, x + 1]
        lower_x = vpad[:, x]
        upper_x = vpad[:, x + 2]
        lower_y = jnp.where(line == 0, y_in[0, :, x], pltpu.roll(center, 1, 1))
        upper_y = jnp.where(line == cy - 1, y_in[1, :, x], pltpu.roll(center, cy - 1, 1))
        here = spot + x == spot_lane
        low_z = jnp.sum(jnp.where(here, z_in[0][None], 0.0), axis=2, keepdims=True)
        high_z = jnp.sum(jnp.where(here, z_in[1][None], 0.0), axis=2, keepdims=True)
        lower_z = jnp.where(lane == 0, low_z, pltpu.roll(center, 1, 2))
        upper_z = jnp.where(lane == cz - 1, high_z, pltpu.roll(center, cz - 1, 2))
        divergence = 0.5 * (
            upper_x * upper_x[0:1] - lower_x * lower_x[0:1]
            + upper_y * upper_y[1:2] - lower_y * lower_y[1:2]
            + upper_z * upper_z[2:3] - lower_z * lower_z[2:3]
        )
        laplace = upper_x + lower_x + upper_y + lower_y + upper_z + lower_z - 6.0 * center
        out[:, x] = center + time_step * (diffusion * laplace - divergence)
        return carry

    lax.fori_loop(0, cx, step, 0)

    own.wait()

    def arrived(k, carry):
        g, device = partner(k)
        pltpu.make_async_remote_copy(
            src_ref=eddy.at[g], dst_ref=recv.at[g], send_sem=send_sem.at[g],
            recv_sem=recv_sem.at[g], device_id=device, device_id_type=MESH,
        ).wait_recv()
        return carry

    lax.fori_loop(1, groups, arrived, 0)

    high, low = halves(recv[...].reshape(total, width))
    visc = dot(place, high, ((1,), (0,))) + dot(place, low, ((1,), (0,)))
    visc = jnp.transpose(visc).reshape(2, width // 2, rows)
    stress = wall_solve(visc, w.reshape(2, width // 2, rows))
    stress_out[...] = stress

    at_xy = lax.broadcasted_iota(jnp.int32, (cx * cy, rows), 0) == cell_xy
    for c in range(2):
        high, low = halves(jnp.where(at_xy, wall_gain * stress[c : c + 1], 0.0))
        forcing = dot(high, at_z, ((1,), (1,))) + dot(low, at_z, ((1,), (1,)))
        out[c] = out[c] - forcing.reshape(cx, cy, cz)

    for leaves, _, copy, _ in sides:
        pl.when(leaves)(copy.wait_send)

    def sent(k, carry):
        eddy_copy(k).wait_send()
        return carry

    lax.fori_loop(1, groups, sent, 0)


def shards(sizes, velocity, probe, eddy, slot_row, row_cell):
    groups, capacity = slot_row.shape
    rows, width = probe.shape
    _, cx, cy, cz = velocity.shape
    if capacity % 8:
        slot_row = slot_row.reshape(1, groups * capacity)
    f32 = jnp.float32
    vmem = pl.BlockSpec(memory_space=pltpu.VMEM)
    hbm = pl.BlockSpec(memory_space=pltpu.HBM)
    return pl.pallas_call(
        functools.partial(kernel, sizes),
        out_shape=(
            pltpu.VMEM(velocity.shape, f32),
            pltpu.VMEM((2, rows), f32),
        ),
        in_specs=[hbm] * 5,
        out_specs=(vmem, vmem),
        scratch_shapes=[
            pltpu.VMEM((3, cx + 2, cy, cz), f32),
            pltpu.VMEM((groups, capacity, width), f32),
            pltpu.VMEM((rows, width), f32),
            pltpu.VMEM(slot_row.shape, jnp.int32),
            pltpu.VMEM((1, rows), jnp.int32),
            pltpu.VMEM((2, 3, cx, 1, cz), f32),
            pltpu.VMEM((2, 3, cx, 1, cz), f32),
            pltpu.VMEM((2, cy, 128), f32),
            pltpu.VMEM((2, cy, 128), f32),
            pltpu.SemaphoreType.DMA((groups,)),
            pltpu.SemaphoreType.DMA((groups,)),
            pltpu.SemaphoreType.DMA((6,)),
            pltpu.SemaphoreType.DMA((6,)),
            pltpu.SemaphoreType.DMA((5,)),
        ],
        compiler_params=pltpu.CompilerParams(
            collective_id=0, has_side_effects=True
        ),
    )(velocity, probe, eddy.reshape(groups, capacity, width), slot_row, row_cell.reshape(1, rows))


def solution(mesh):
    in_specs = (
        P(None, "stream", "span", "radial"),
        P(("stream", "span", "radial"), None),
        P(("stream", "span", "radial"), None),
        P(("stream", "span", "radial"), None),
        P(("stream", "span", "radial")),
    )
    out_specs = (P(None, "stream", "span", "radial"), P(None, ("stream", "span", "radial")))
    sizes = tuple(mesh.shape[a] for a in ("stream", "span", "radial"))
    return jax.shard_map(
        functools.partial(shards, sizes), mesh=mesh, in_specs=in_specs, out_specs=out_specs, check_vma=False
    )
```

```python
import functools
import jax
import jax.numpy as jnp
from jax import lax
from jax.experimental import pallas as pl
from jax.experimental.pallas import tpu as pltpu
from jax.sharding import PartitionSpec as P

ITERS = 6

source_gain = 0.00390625
relaxation = 0.8
time_step = 0.1
diffusion = 0.5
wall_gain = 0.25

MESH = pl.DeviceIdType.MESH


def halves(x):
    high = x.astype(jnp.bfloat16)
    return high, (x - high.astype(jnp.float32)).astype(jnp.bfloat16)


def dot(a, b, dims):
    return lax.dot_general(a, b, (dims, ((), ())), preferred_element_type=jnp.float32)


def suffix_sums(samples):
    width = samples.shape[1]
    points = width // 2
    row = lax.broadcasted_iota(jnp.int32, (width, width), 0)
    col = lax.broadcasted_iota(jnp.int32, (width, width), 1)
    keep = (col >= row) & ((col >= points) == (row >= points))
    table = jnp.where(keep, source_gain, 0.0).astype(jnp.bfloat16)
    high, low = halves(samples)
    return dot(table, high, ((1,), (1,))) + dot(table, low, ((1,), (1,)))


def wall_solve(visc, w):
    points, count = visc.shape[1], visc.shape[1] + 1
    v_top = visc[:, points - 1 : points]
    w_top = -(v_top * (w[:, points - 1 : points] * (1.0 / source_gain)))
    u, u_top = w, w_top
    d = jnp.zeros_like(w)
    d_top = jnp.zeros_like(w_top)
    for sweep in range(ITERS):
        mean = (jnp.sum(u, axis=1, keepdims=True) + u_top) * (1.0 / count)
        if sweep == ITERS - 1:
            first = d[:, 0:1] + relaxation * (u[:, 0:1] - mean)
            return (count * visc[:, 0:1] * first)[:, 0]
        d = d + relaxation * (u - mean)
        d_top = d_top + relaxation * (u_top - mean)
        u = w - visc * d
        u_top = w_top - v_top * d_top


def kernel(
    sizes, vel, probe_far, eddy, slots_far, cells_far, out, stress_out,
    vpad, recv, probe, slots, cells, y_out, y_in, z_out, z_in,
    send_sem, recv_sem, halo_send, halo_recv, local_sem,
):
    n_stream, n_span, n_radial = sizes
    s, p, r = (lax.axis_index(a) for a in ("stream", "span", "radial"))
    groups, capacity, width = eddy.shape
    _, cx, cy, cz = vel.shape
    me = s * n_span + p

    def partner(k):
        g = lax.rem(me + k, groups)
        return g, (lax.div(g, n_span), lax.rem(g, n_span), r)

    load = pltpu.make_async_copy(vel, vpad.at[:, pl.ds(1, cx)], local_sem.at[0])
    load.start()
    smalls = [
        pltpu.make_async_copy(far, near, local_sem.at[2 + i])
        for i, (far, near) in enumerate(((probe_far, probe), (slots_far, slots), (cells_far, cells)))
    ]
    for copy in smalls:
        copy.start()
    own = pltpu.make_async_copy(eddy.at[me], recv.at[me], local_sem.at[1])
    own.start()

    barrier = pltpu.get_barrier_semaphore()

    def greet(k, carry):
        pl.semaphore_signal(barrier, inc=1, device_id=partner(k)[1], device_id_type=MESH)
        return carry

    lax.fori_loop(1, groups, greet, 0)

    for radial in (lax.rem(r + 1, n_radial), lax.rem(r + n_radial - 1, n_radial)):
        pl.semaphore_signal(barrier, inc=1, device_id=(s, p, radial), device_id_type=MESH)
    load.wait()
    y_out[0] = vpad[:, 1 : cx + 1, cy - 1 : cy, :]
    y_out[1] = vpad[:, 1 : cx + 1, 0:1, :]
    lanes = z_out.shape[2]
    shape4 = (3, cx, cy, lanes)
    plane = lax.broadcasted_iota(jnp.int32, shape4, 0) * cx + lax.broadcasted_iota(jnp.int32, shape4, 1)
    picked = plane == lax.broadcasted_iota(jnp.int32, shape4, 3)
    for i, column in ((0, cz - 1), (1, 0)):
        face = jnp.where(picked, vpad[:, 1 : cx + 1, :, column : column + 1], 0.0)
        z_out[i] = jnp.sum(jnp.sum(face, axis=0), axis=0)

    def face_copy(i, src, dst, device):
        return pltpu.make_async_remote_copy(
            src_ref=src, dst_ref=dst, send_sem=halo_send.at[i],
            recv_sem=halo_recv.at[i], device_id=device, device_id_type=MESH,
        )

    sides = [
        (s < n_stream - 1, s > 0, face_copy(0, vpad.at[:, cx], vpad.at[:, 0], (s + 1, p, r)), vpad.at[:, 0]),
        (s > 0, s < n_stream - 1, face_copy(1, vpad.at[:, 1], vpad.at[:, cx + 1], (s - 1, p, r)), vpad.at[:, cx + 1]),
        (p < n_span - 1, p > 0, face_copy(2, y_out.at[0], y_in.at[0], (s, p + 1, r)), y_in.at[0]),
        (p > 0, p < n_span - 1, face_copy(3, y_out.at[1], y_in.at[1], (s, p - 1, r)), y_in.at[1]),
        (r < n_radial - 1, r > 0, face_copy(4, z_out.at[0], z_in.at[0], (s, p, r + 1)), z_in.at[0]),
        (r > 0, r < n_radial - 1, face_copy(5, z_out.at[1], z_in.at[1], (s, p, r - 1)), z_in.at[1]),
    ]
    for _, arrives, _, ref in sides:
        @pl.when(jnp.logical_not(arrives))
        def _():
            ref[...] = jnp.zeros(ref.shape, ref.dtype)

    pl.semaphore_wait(barrier, groups + 1)

    def eddy_copy(k):
        g, device = partner(k)
        return pltpu.make_async_remote_copy(
            src_ref=eddy.at[g], dst_ref=recv.at[me], send_sem=send_sem.at[g],
            recv_sem=recv_sem.at[me], device_id=device, device_id_type=MESH,
        )

    def send(k, carry):
        eddy_copy(k).start()
        return carry

    for leaves, _, copy, _ in sides[2:]:
        pl.when(leaves)(copy.start)
    lax.fori_loop(1, groups, send, 0)
    for leaves, _, copy, _ in sides[:2]:
        pl.when(leaves)(copy.start)

    rows = probe.shape[0]
    for copy in smalls:
        copy.wait()
    w = suffix_sums(probe[...])
    if slots.shape[0] == 1:
        slot_line = slots[...]
    else:
        slot_line = jnp.concatenate([slots[g : g + 1, :] for g in range(groups)], axis=1)
    total = groups * capacity
    place = (lax.broadcasted_iota(jnp.int32, (rows, total), 0) == slot_line).astype(jnp.float32).astype(jnp.bfloat16)
    cell = cells[...]
    cell_z = lax.rem(cell, cz)
    cell_xy = lax.div(cell, cz)
    at_z = (lax.broadcasted_iota(jnp.int32, (cz, rows), 0) == cell_z).astype(jnp.float32).astype(jnp.bfloat16)

    for _, arrives, copy, _ in sides[2:]:
        pl.when(arrives)(copy.wait_recv)

    line = lax.broadcasted_iota(jnp.int32, (3, cy, cz), 1)
    lane = lax.broadcasted_iota(jnp.int32, (3, cy, cz), 2)
    spot = lax.broadcasted_iota(jnp.int32, (3, cy, lanes), 0) * cx
    spot_lane = lax.broadcasted_iota(jnp.int32, (3, cy, lanes), 2)

    def step(x, carry):
        center = vpad[:, x + 1]
        lower_x = vpad[:, x]
        upper_x = vpad[:, x + 2]
        lower_y = jnp.where(line == 0, y_in[0, :, x], pltpu.roll(center, 1, 1))
        upper_y = jnp.where(line == cy - 1, y_in[1, :, x], pltpu.roll(center, cy - 1, 1))
        here = spot + x == spot_lane
        low_z = jnp.sum(jnp.where(here, z_in[0][None], 0.0), axis=2, keepdims=True)
        high_z = jnp.sum(jnp.where(here, z_in[1][None], 0.0), axis=2, keepdims=True)
        lower_z = jnp.where(lane == 0, low_z, pltpu.roll(center, 1, 2))
        upper_z = jnp.where(lane == cz - 1, high_z, pltpu.roll(center, cz - 1, 2))
        divergence = 0.5 * (
            upper_x * upper_x[0:1] - lower_x * lower_x[0:1]
            + upper_y * upper_y[1:2] - lower_y * lower_y[1:2]
            + upper_z * upper_z[2:3] - lower_z * lower_z[2:3]
        )
        laplace = upper_x + lower_x + upper_y + lower_y + upper_z + lower_z - 6.0 * center
        out[:, x] = center + time_step * (diffusion * laplace - divergence)
        return carry

    lax.fori_loop(1, cx - 1, step, 0)
    for _, arrives, copy, _ in sides[:2]:
        pl.when(arrives)(copy.wait_recv)
    lax.fori_loop(0, 2, lambda i, carry: step(i * (cx - 1), carry), 0)

    own.wait()

    def arrived(k, carry):
        g, device = partner(k)
        pltpu.make_async_remote_copy(
            src_ref=eddy.at[g], dst_ref=recv.at[g], send_sem=send_sem.at[g],
            recv_sem=recv_sem.at[g], device_id=device, device_id_type=MESH,
        ).wait_recv()
        return carry

    lax.fori_loop(1, groups, arrived, 0)

    high, low = halves(recv[...].reshape(total, width))
    visc = dot(place, high, ((1,), (0,))) + dot(place, low, ((1,), (0,)))
    visc = jnp.transpose(visc).reshape(2, width // 2, rows)
    stress = wall_solve(visc, w.reshape(2, width // 2, rows))
    stress_out[...] = stress

    at_xy = lax.broadcasted_iota(jnp.int32, (cx * cy, rows), 0) == cell_xy
    for c in range(2):
        high, low = halves(jnp.where(at_xy, wall_gain * stress[c : c + 1], 0.0))
        forcing = dot(high, at_z, ((1,), (1,))) + dot(low, at_z, ((1,), (1,)))
        out[c] = out[c] - forcing.reshape(cx, cy, cz)

    for leaves, _, copy, _ in sides:
        pl.when(leaves)(copy.wait_send)

    def sent(k, carry):
        eddy_copy(k).wait_send()
        return carry

    lax.fori_loop(1, groups, sent, 0)


def write_out(first, second, first_out, second_out, sem):
    copies = [
        pltpu.make_async_copy(first, first_out, sem.at[0]),
        pltpu.make_async_copy(second, second_out, sem.at[1]),
    ]
    for copy in copies:
        copy.start()
    for copy in copies:
        copy.wait()


def shards(sizes, velocity, probe, eddy, slot_row, row_cell):
    groups, capacity = slot_row.shape
    rows, width = probe.shape
    _, cx, cy, cz = velocity.shape
    if capacity % 8:
        slot_row = slot_row.reshape(1, groups * capacity)
    f32 = jnp.float32
    vmem = pl.BlockSpec(memory_space=pltpu.VMEM)
    hbm = pl.BlockSpec(memory_space=pltpu.HBM)
    results = pl.pallas_call(
        functools.partial(kernel, sizes),
        out_shape=(
            pltpu.VMEM(velocity.shape, f32),
            pltpu.VMEM((2, rows), f32),
        ),
        in_specs=[hbm] * 5,
        out_specs=(vmem, vmem),
        scratch_shapes=[
            pltpu.VMEM((3, cx + 2, cy, cz), f32),
            pltpu.VMEM((groups, capacity, width), f32),
            pltpu.VMEM((rows, width), f32),
            pltpu.VMEM(slot_row.shape, jnp.int32),
            pltpu.VMEM((1, rows), jnp.int32),
            pltpu.VMEM((2, 3, cx, 1, cz), f32),
            pltpu.VMEM((2, 3, cx, 1, cz), f32),
            pltpu.VMEM((2, cy, 128), f32),
            pltpu.VMEM((2, cy, 128), f32),
            pltpu.SemaphoreType.DMA((groups,)),
            pltpu.SemaphoreType.DMA((groups,)),
            pltpu.SemaphoreType.DMA((6,)),
            pltpu.SemaphoreType.DMA((6,)),
            pltpu.SemaphoreType.DMA((5,)),
        ],
        compiler_params=pltpu.CompilerParams(
            collective_id=0, has_side_effects=True
        ),
    )(velocity, probe, eddy.reshape(groups, capacity, width), slot_row, row_cell.reshape(1, rows))
    return pl.pallas_call(
        write_out,
        out_shape=(
            jax.ShapeDtypeStruct(velocity.shape, f32),
            jax.ShapeDtypeStruct((2, rows), f32),
        ),
        in_specs=[pl.BlockSpec(memory_space=pl.ANY)] * 2,
        out_specs=(hbm, hbm),
        scratch_shapes=[pltpu.SemaphoreType.DMA((2,))],
        compiler_params=pltpu.CompilerParams(vmem_limit_bytes=2 * 1024 * 1024),
    )(*results)


def solution(mesh):
    in_specs = (
        P(None, "stream", "span", "radial"),
        P(("stream", "span", "radial"), None),
        P(("stream", "span", "radial"), None),
        P(("stream", "span", "radial"), None),
        P(("stream", "span", "radial")),
    )
    out_specs = (P(None, "stream", "span", "radial"), P(None, ("stream", "span", "radial")))
    sizes = tuple(mesh.shape[a] for a in ("stream", "span", "radial"))
    return jax.shard_map(
        functools.partial(shards, sizes), mesh=mesh, in_specs=in_specs, out_specs=out_specs, check_vma=False
    )
```

```python
import functools
import jax
import jax.numpy as jnp
from jax import lax
from jax.experimental import pallas as pl
from jax.experimental.pallas import tpu as pltpu
from jax.sharding import PartitionSpec as P

ITERS = 6

source_gain = 0.00390625
relaxation = 0.8
time_step = 0.1
diffusion = 0.5
wall_gain = 0.25

MESH = pl.DeviceIdType.MESH


def halves(x):
    high = x.astype(jnp.bfloat16)
    return high, (x - high.astype(jnp.float32)).astype(jnp.bfloat16)


def dot(a, b, dims):
    return lax.dot_general(a, b, (dims, ((), ())), preferred_element_type=jnp.float32)


def suffix_sums(samples):
    width = samples.shape[1]
    points = width // 2
    row = lax.broadcasted_iota(jnp.int32, (width, width), 0)
    col = lax.broadcasted_iota(jnp.int32, (width, width), 1)
    keep = (col >= row) & ((col >= points) == (row >= points))
    table = jnp.where(keep, source_gain, 0.0).astype(jnp.bfloat16)
    high, low = halves(samples)
    return dot(table, high, ((1,), (1,))) + dot(table, low, ((1,), (1,)))


def wall_solve(visc, w):
    points, count = visc.shape[1], visc.shape[1] + 1
    v_top = visc[:, points - 1 : points]
    w_top = -(v_top * (w[:, points - 1 : points] * (1.0 / source_gain)))
    u, u_top = w, w_top
    d = jnp.zeros_like(w)
    d_top = jnp.zeros_like(w_top)
    for sweep in range(ITERS):
        mean = (jnp.sum(u, axis=1, keepdims=True) + u_top) * (1.0 / count)
        if sweep == ITERS - 1:
            first = d[:, 0:1] + relaxation * (u[:, 0:1] - mean)
            return (count * visc[:, 0:1] * first)[:, 0]
        d = d + relaxation * (u - mean)
        d_top = d_top + relaxation * (u_top - mean)
        u = w - visc * d
        u_top = w_top - v_top * d_top


def kernel(
    sizes, vel, probe_far, eddy, slots_far, cells_far, out, stress_out,
    vpad, recv, probe, slots, cells, y_out, y_in, z_out, z_in,
    send_sem, recv_sem, halo_send, halo_recv, local_sem,
):
    n_stream, n_span, n_radial = sizes
    s, p, r = (lax.axis_index(a) for a in ("stream", "span", "radial"))
    groups, capacity, width = eddy.shape
    _, cx, cy, cz = vel.shape
    me = s * n_span + p

    def partner(k):
        g = lax.rem(me + k, groups)
        return g, (lax.div(g, n_span), lax.rem(g, n_span), r)

    load = pltpu.make_async_copy(vel, vpad.at[:, pl.ds(1, cx)], local_sem.at[0])
    load.start()
    smalls = [
        pltpu.make_async_copy(far, near, local_sem.at[2 + i])
        for i, (far, near) in enumerate(((probe_far, probe), (slots_far, slots), (cells_far, cells)))
    ]
    for copy in smalls:
        copy.start()
    own = pltpu.make_async_copy(eddy.at[me], recv.at[me], local_sem.at[1])
    own.start()

    barrier = pltpu.get_barrier_semaphore()

    def greet(k, carry):
        pl.semaphore_signal(barrier, inc=1, device_id=partner(k)[1], device_id_type=MESH)
        return carry

    lax.fori_loop(1, groups, greet, 0)

    for radial in (lax.rem(r + 1, n_radial), lax.rem(r + n_radial - 1, n_radial)):
        pl.semaphore_signal(barrier, inc=1, device_id=(s, p, radial), device_id_type=MESH)
    load.wait()
    y_out[0] = vpad[:, 1 : cx + 1, cy - 1 : cy, :]
    y_out[1] = vpad[:, 1 : cx + 1, 0:1, :]
    lanes = z_out.shape[2]
    shape4 = (3, cx, cy, lanes)
    plane = lax.broadcasted_iota(jnp.int32, shape4, 0) * cx + lax.broadcasted_iota(jnp.int32, shape4, 1)
    picked = plane == lax.broadcasted_iota(jnp.int32, shape4, 3)
    for i, column in ((0, cz - 1), (1, 0)):
        face = jnp.where(picked, vpad[:, 1 : cx + 1, :, column : column + 1], 0.0)
        z_out[i] = jnp.sum(jnp.sum(face, axis=0), axis=0)

    def face_copy(i, src, dst, device):
        return pltpu.make_async_remote_copy(
            src_ref=src, dst_ref=dst, send_sem=halo_send.at[i],
            recv_sem=halo_recv.at[i], device_id=device, device_id_type=MESH,
        )

    sides = [
        (s < n_stream - 1, s > 0, face_copy(0, vpad.at[:, cx], vpad.at[:, 0], (s + 1, p, r)), vpad.at[:, 0]),
        (s > 0, s < n_stream - 1, face_copy(1, vpad.at[:, 1], vpad.at[:, cx + 1], (s - 1, p, r)), vpad.at[:, cx + 1]),
        (p < n_span - 1, p > 0, face_copy(2, y_out.at[0], y_in.at[0], (s, p + 1, r)), y_in.at[0]),
        (p > 0, p < n_span - 1, face_copy(3, y_out.at[1], y_in.at[1], (s, p - 1, r)), y_in.at[1]),
        (r < n_radial - 1, r > 0, face_copy(4, z_out.at[0], z_in.at[0], (s, p, r + 1)), z_in.at[0]),
        (r > 0, r < n_radial - 1, face_copy(5, z_out.at[1], z_in.at[1], (s, p, r - 1)), z_in.at[1]),
    ]
    for _, arrives, _, ref in sides:
        @pl.when(jnp.logical_not(arrives))
        def _():
            ref[...] = jnp.zeros(ref.shape, ref.dtype)

    rows = probe.shape[0]
    for copy in smalls:
        copy.wait()
    w = suffix_sums(probe[...])
    if slots.shape[0] == 1:
        slot_line = slots[...]
    else:
        slot_line = jnp.concatenate([slots[g : g + 1, :] for g in range(groups)], axis=1)
    total = groups * capacity
    place = (lax.broadcasted_iota(jnp.int32, (rows, total), 0) == slot_line).astype(jnp.float32).astype(jnp.bfloat16)
    cell = cells[...]
    cell_z = lax.rem(cell, cz)
    cell_xy = lax.div(cell, cz)
    at_z = (lax.broadcasted_iota(jnp.int32, (cz, rows), 0) == cell_z).astype(jnp.float32).astype(jnp.bfloat16)

    pl.semaphore_wait(barrier, groups + 1)

    def eddy_copy(k):
        g, device = partner(k)
        return pltpu.make_async_remote_copy(
            src_ref=eddy.at[g], dst_ref=recv.at[me], send_sem=send_sem.at[g],
            recv_sem=recv_sem.at[me], device_id=device, device_id_type=MESH,
        )

    def send(k, carry):
        eddy_copy(k).start()
        return carry

    for leaves, _, copy, _ in sides[2:]:
        pl.when(leaves)(copy.start)
    if groups == 8:
        for k in (2, 1, 3, 4, 6, 5, 7):
            send(k, 0)
    else:
        lax.fori_loop(1, groups, send, 0)
    for leaves, _, copy, _ in sides[:2]:
        pl.when(leaves)(copy.start)

    for _, arrives, copy, _ in sides[2:]:
        pl.when(arrives)(copy.wait_recv)

    line = lax.broadcasted_iota(jnp.int32, (3, cy, cz), 1)
    lane = lax.broadcasted_iota(jnp.int32, (3, cy, cz), 2)
    spot = lax.broadcasted_iota(jnp.int32, (3, cy, lanes), 0) * cx
    spot_lane = lax.broadcasted_iota(jnp.int32, (3, cy, lanes), 2)

    def step(x, carry):
        center = vpad[:, x + 1]
        lower_x = vpad[:, x]
        upper_x = vpad[:, x + 2]
        lower_y = jnp.where(line == 0, y_in[0, :, x], pltpu.roll(center, 1, 1))
        upper_y = jnp.where(line == cy - 1, y_in[1, :, x], pltpu.roll(center, cy - 1, 1))
        here = spot + x == spot_lane
        low_z = jnp.sum(jnp.where(here, z_in[0][None], 0.0), axis=2, keepdims=True)
        high_z = jnp.sum(jnp.where(here, z_in[1][None], 0.0), axis=2, keepdims=True)
        lower_z = jnp.where(lane == 0, low_z, pltpu.roll(center, 1, 2))
        upper_z = jnp.where(lane == cz - 1, high_z, pltpu.roll(center, cz - 1, 2))
        divergence = 0.5 * (
            upper_x * upper_x[0:1] - lower_x * lower_x[0:1]
            + upper_y * upper_y[1:2] - lower_y * lower_y[1:2]
            + upper_z * upper_z[2:3] - lower_z * lower_z[2:3]
        )
        laplace = upper_x + lower_x + upper_y + lower_y + upper_z + lower_z - 6.0 * center
        out[:, x] = center + time_step * (diffusion * laplace - divergence)
        return carry

    lax.fori_loop(1, cx - 1, step, 0)
    for _, arrives, copy, _ in sides[:2]:
        pl.when(arrives)(copy.wait_recv)
    lax.fori_loop(0, 2, lambda i, carry: step(i * (cx - 1), carry), 0)

    own.wait()

    def arrived(k, carry):
        g, device = partner(k)
        pltpu.make_async_remote_copy(
            src_ref=eddy.at[g], dst_ref=recv.at[g], send_sem=send_sem.at[g],
            recv_sem=recv_sem.at[g], device_id=device, device_id_type=MESH,
        ).wait_recv()
        return carry

    lax.fori_loop(1, groups, arrived, 0)

    high, low = halves(recv[...].reshape(total, width))
    visc = dot(place, high, ((1,), (0,))) + dot(place, low, ((1,), (0,)))
    visc = jnp.transpose(visc).reshape(2, width // 2, rows)
    stress = wall_solve(visc, w.reshape(2, width // 2, rows))
    stress_out[...] = stress

    at_xy = lax.broadcasted_iota(jnp.int32, (cx * cy, rows), 0) == cell_xy
    for c in range(2):
        high, low = halves(jnp.where(at_xy, wall_gain * stress[c : c + 1], 0.0))
        forcing = dot(high, at_z, ((1,), (1,))) + dot(low, at_z, ((1,), (1,)))
        out[c] = out[c] - forcing.reshape(cx, cy, cz)

    for leaves, _, copy, _ in sides:
        pl.when(leaves)(copy.wait_send)

    def sent(k, carry):
        eddy_copy(k).wait_send()
        return carry

    lax.fori_loop(1, groups, sent, 0)


def write_out(first, second, first_out, second_out, sem):
    copies = [
        pltpu.make_async_copy(first, first_out, sem.at[0]),
        pltpu.make_async_copy(second, second_out, sem.at[1]),
    ]
    for copy in copies:
        copy.start()
    for copy in copies:
        copy.wait()


def shards(sizes, velocity, probe, eddy, slot_row, row_cell):
    groups, capacity = slot_row.shape
    rows, width = probe.shape
    _, cx, cy, cz = velocity.shape
    if capacity % 8:
        slot_row = slot_row.reshape(1, groups * capacity)
    f32 = jnp.float32
    vmem = pl.BlockSpec(memory_space=pltpu.VMEM)
    hbm = pl.BlockSpec(memory_space=pltpu.HBM)
    results = pl.pallas_call(
        functools.partial(kernel, sizes),
        out_shape=(
            pltpu.VMEM(velocity.shape, f32),
            pltpu.VMEM((2, rows), f32),
        ),
        in_specs=[hbm] * 5,
        out_specs=(vmem, vmem),
        scratch_shapes=[
            pltpu.VMEM((3, cx + 2, cy, cz), f32),
            pltpu.VMEM((groups, capacity, width), f32),
            pltpu.VMEM((rows, width), f32),
            pltpu.VMEM(slot_row.shape, jnp.int32),
            pltpu.VMEM((1, rows), jnp.int32),
            pltpu.VMEM((2, 3, cx, 1, cz), f32),
            pltpu.VMEM((2, 3, cx, 1, cz), f32),
            pltpu.VMEM((2, cy, 128), f32),
            pltpu.VMEM((2, cy, 128), f32),
            pltpu.SemaphoreType.DMA((groups,)),
            pltpu.SemaphoreType.DMA((groups,)),
            pltpu.SemaphoreType.DMA((6,)),
            pltpu.SemaphoreType.DMA((6,)),
            pltpu.SemaphoreType.DMA((5,)),
        ],
        compiler_params=pltpu.CompilerParams(
            collective_id=0, has_side_effects=True
        ),
    )(velocity, probe, eddy.reshape(groups, capacity, width), slot_row, row_cell.reshape(1, rows))
    return pl.pallas_call(
        write_out,
        out_shape=(
            jax.ShapeDtypeStruct(velocity.shape, f32),
            jax.ShapeDtypeStruct((2, rows), f32),
        ),
        in_specs=[pl.BlockSpec(memory_space=pl.ANY)] * 2,
        out_specs=(hbm, hbm),
        scratch_shapes=[pltpu.SemaphoreType.DMA((2,))],
        compiler_params=pltpu.CompilerParams(vmem_limit_bytes=2 * 1024 * 1024),
    )(*results)


def solution(mesh):
    in_specs = (
        P(None, "stream", "span", "radial"),
        P(("stream", "span", "radial"), None),
        P(("stream", "span", "radial"), None),
        P(("stream", "span", "radial"), None),
        P(("stream", "span", "radial")),
    )
    out_specs = (P(None, "stream", "span", "radial"), P(None, ("stream", "span", "radial")))
    sizes = tuple(mesh.shape[a] for a in ("stream", "span", "radial"))
    return jax.shard_map(
        functools.partial(shards, sizes), mesh=mesh, in_specs=in_specs, out_specs=out_specs, check_vma=False
    )
```
